32 devices in a mesh: sys: 2 (over x), box: 16 (over z, y, core).
Axes of the slice: x: 2, y: 2, z: 4, core: 2. Of those that a mesh axis runs over, the one named last changes fastest.
Arguments:
- charges: bfloat16 [16, 131072], P(None, ('sys', 'box')), parts along dimension 1, may hold values from -6 to 6
- harmonics: bfloat16 [121, 131072], P(None, ('sys', 'box')), parts along dimension 1, may hold values from -0.59765625 to 0.59765625
- counts: int32 [256], P(('sys', 'box')), parts along dimension 0, may hold values from 128 to 512, as said below
- m2l_ops: bfloat16 [121, 22869], replicated, may hold values from -0.0390625 to 0.0390625
- m2m_ops: bfloat16 [8, 121, 121], replicated, may hold values from -0.1875 to 0.1875
- l2l_ops: bfloat16 [8, 121, 121], replicated, may hold values from -0.5 to 0.5
- sources: int32 [189, 256], P(None, ('sys', 'box')), parts along dimension 1, may hold values from 0 to 127, as said below
- list_mask: int32 [189, 256], P(None, ('sys', 'box')), parts along dimension 1, may hold values 0 or 1
- top_sources: int32 [32, 32], P('sys'), parts along dimension 0, may hold values from 0 to 15
- top_vectors: int32 [32, 32], P('sys'), parts along dimension 0, may hold values from 0 to 188
- neighbours: int32 [32, 131072], P(None, ('sys', 'box')), parts along dimension 1, may hold values from 0 to 6143, as said below
- edge_weights: bfloat16 [32, 131072], P(None, ('sys', 'box')), parts along dimension 1, may hold values from -1 to 1
Outputs:
- potential: bfloat16 [16, 131072], P(None, ('sys', 'box')), parts along dimension 1
The draws below stay inside these ranges and needn't reach their ends.
There are 2 independent parts, one for each index of `sys`. The reference program is written for one: setup_inputs(seed, part) draws one part's arguments, and reference() takes and returns one part's arrays. A program takes and returns all parts, laid end to end along the dimension named above; an argument that names none is the same for every part. Nothing has to cross between parts.
Inputs may be any that keep to these rules, and one draw needn't show every extreme that they name: `counts`: each leaf holds 128 to 512 atoms; every device's range of leaves has a full one. sources[v, t] lies in the leaves from (t // 8 - 1) * 8 to (t // 8 + 2) * 8 - 1; both ends are reached in every range where they exist. `neighbours`: both ends of the window are reached in every device's range of atoms.
All inputs are finite; a program needn't handle non-finite values. No bound on the sum of `list_mask` on one device may be relied on, other than what follows from the above.
Results may differ from the reference program's by a relative error of at most 0.003.
Values may be sent and summed in bfloat16 or wider, within the bound.
A program may use at most 128 MiB of HBM per device.

```python
import jax
import jax.numpy as jnp
from jax import lax

C = 16
NCOEF = 121
NVEC = 189
BOX_DEV = 8
CAP = 512
NB = 32
CLIST = 32
TOPS = 16
BOXES = 128
ATOM_DEV = 4096
ATOMS = 65536
GHOST = 1024


def draw_counts(key, part):
    key_base, key_full = jax.random.split(jax.random.fold_in(key, 11))
    base = jax.random.randint(key_base, (BOXES,), CAP // 4, CAP + 1)
    full_slot = jax.random.randint(key_full, (TOPS,), 0, BOX_DEV)
    leaves = jnp.arange(BOXES)
    is_full = leaves % BOX_DEV == full_slot[leaves // BOX_DEV]
    return jnp.where(is_full, CAP, base).astype(jnp.int32)


def banded(key, rows, total, per_dev, reach):
    target = jnp.arange(total)
    owner = target // per_dev
    offset = jax.random.randint(key, (rows, total), -reach, per_dev + reach)
    row_id = jnp.arange(rows)[:, None]
    low_end = (target % per_dev == 0)[None]
    high_end = (target % per_dev == per_dev - 1)[None]
    offset = jnp.where((row_id == 0) & low_end, -reach, offset)
    offset = jnp.where((row_id == rows - 1) & high_end, per_dev + reach - 1, offset)
    return jnp.clip(owner[None] * per_dev + offset, 0, total - 1).astype(jnp.int32)


def draw_sources(key, part):
    return banded(jax.random.fold_in(key, 23), NVEC, BOXES, BOX_DEV, BOX_DEV)


def draw_neighbours(key, part):
    span = ATOM_DEV + 2 * GHOST
    local = jax.random.randint(jax.random.fold_in(key, 37), (NB, ATOMS), 0, span)
    within = jnp.arange(ATOMS) % ATOM_DEV
    row_id = jnp.arange(NB)[:, None]
    local = jnp.where((row_id == 0) & (within == 0)[None], 0, local)
    local = jnp.where((row_id == NB - 1) & (within == ATOM_DEV - 1)[None], span - 1, local)
    return local.astype(jnp.int32)


def plant(entries, stream_key, smallest, top_value):
    longest = entries.shape.index(max(entries.shape))
    spots = []
    for shift in (0, 1):
        where = [jax.random.randint(jax.random.fold_in(stream_key, axis), (), 0, length) for axis, length in enumerate(entries.shape)]
        where[longest] = (where[longest] + shift) % entries.shape[longest]
        spots.append(tuple(where))
    return entries.at[spots[0]].set(smallest).at[spots[1]].set(top_value)


def steps_of(key, extent, shards, least, top_value):
    level, own = 1.0, jax.random.fold_in(key, 6)
    for dim, shards_of in shards:
        steps = jnp.exp(jax.random.uniform(jax.random.fold_in(own, dim), (shards_of,), jnp.float32, least / len(shards), top_value / len(shards)))
        level = level * jnp.repeat(steps, extent[dim] // shards_of).reshape([-1 if axis == dim else 1 for axis in range(len(extent))])
    return level


def noise(rng, dims, deviation, most, cuts=(), kind=jnp.bfloat16):
    level = steps_of(rng, dims, cuts, -0.22, 0.18) if cuts else 1.0
    values = jax.random.normal(rng, dims, jnp.float32) * deviation * level
    return jnp.minimum(jnp.maximum(values, -most), most).astype(kind)


def setup_inputs(seed: int = 0, part: int = 0) -> dict:
    key_of = jax.random.split(jax.random.key(seed), 13)
    own_keys = jax.random.split(jax.random.fold_in(key_of[12], part), 13)
    charges = noise(own_keys[0], (C, ATOMS), 1.0, 6.0, ((1, 16),))
    harmonics = noise(own_keys[1], (NCOEF, ATOMS), 0.1, 0.59765625, ((1, 16),))
    counts = draw_counts(jax.random.fold_in(jax.random.fold_in(key_of[12], part), 71), part)
    m2l_ops = noise(key_of[3], (NCOEF, NVEC * NCOEF), (NCOEF * NVEC) ** -0.5, 0.0390625)
    m2m_ops = noise(key_of[4], (8, NCOEF, NCOEF), (NCOEF * 8) ** -0.5, 0.1875)
    l2l_ops = noise(key_of[5], (8, NCOEF, NCOEF), NCOEF ** -0.5, 0.5)
    sources = draw_sources(jax.random.fold_in(jax.random.fold_in(key_of[12], part), 71), part)
    list_mask = plant((jax.random.randint(own_keys[7], (NVEC, BOXES), 0, 5) < 4).astype(jnp.int32), jax.random.fold_in(own_keys[7], 1), 0, 1)
    top_sources = plant(jax.random.randint(own_keys[8], (TOPS, CLIST), 0, TOPS), jax.random.fold_in(own_keys[8], 1), 0, TOPS - 1).astype(jnp.int32)
    top_vectors = plant(jax.random.randint(own_keys[9], (TOPS, CLIST), 0, NVEC), jax.random.fold_in(own_keys[9], 1), 0, NVEC - 1).astype(jnp.int32)
    neighbours = draw_neighbours(jax.random.fold_in(jax.random.fold_in(key_of[12], part), 71), part)
    edge_weights = noise(own_keys[11], (NB, ATOMS), NB ** -0.5, 1.0, ((1, 16),))
    return {"charges": charges, "harmonics": harmonics, "counts": counts, "m2l_ops": m2l_ops, "m2m_ops": m2m_ops, "l2l_ops": l2l_ops, "sources": sources, "list_mask": list_mask, "top_sources": top_sources, "top_vectors": top_vectors, "neighbours": neighbours, "edge_weights": edge_weights}


def reference(charges, harmonics, counts, m2l_ops, m2m_ops, l2l_ops, sources, list_mask, top_sources, top_vectors, neighbours, edge_weights):
    live = jnp.arange(CAP, dtype=jnp.int32)[None, :] < counts[:, None]
    masked = jnp.where(live[None], charges.reshape(C, BOXES, CAP), jnp.zeros((), charges.dtype)).astype(jnp.bfloat16)
    harm_box = harmonics.reshape(NCOEF, BOXES, CAP)
    mult = jnp.einsum('kba,cba->kcb', harm_box.astype(jnp.float32), masked.astype(jnp.float32)).astype(jnp.bfloat16)
    level = mult
    while level.shape[2] > TOPS:
        grouped = level.reshape(NCOEF, C, level.shape[2] // 8, 8).astype(jnp.float32)
        level = jnp.einsum('okl,lcpo->kcp', m2m_ops.astype(jnp.float32), grouped).astype(jnp.bfloat16)
    top = level

    def leaf_block(block):
        start = (block * BOX_DEV).astype(jnp.int32)
        index_rows = lax.dynamic_slice_in_dim(sources, start, BOX_DEV, 1)
        mask_rows = lax.dynamic_slice_in_dim(list_mask, start, BOX_DEV, 1).astype(jnp.bfloat16)
        picked = mult[:, :, index_rows] * mask_rows[None, None]
        stacked = picked.transpose(2, 0, 1, 3).reshape(NVEC * NCOEF, C * BOX_DEV)
        return jnp.dot(m2l_ops, stacked, preferred_element_type=jnp.float32).reshape(NCOEF, C, BOX_DEV)

    blocks = lax.map(leaf_block, jnp.arange(TOPS, dtype=jnp.int32))
    leaf_local = blocks.transpose(1, 2, 0, 3).reshape(NCOEF, C, BOXES)

    operators = m2l_ops.reshape(NCOEF, NVEC, NCOEF)
    chosen = operators[:, top_vectors, :].astype(jnp.float32)
    picked_top = top[:, :, top_sources].astype(jnp.float32)
    top_local = jnp.einsum('kejl,lcej->kce', chosen, picked_top).astype(jnp.bfloat16)

    current = top_local
    levels = 0
    width = TOPS
    while width < BOXES:
        width = width * 8
        levels = levels + 1
    for step in range(levels):
        child = jnp.einsum('okl,lcp->kcpo', l2l_ops.astype(jnp.float32), current.astype(jnp.float32))
        child = child.reshape(NCOEF, C, current.shape[2] * 8)
        current = child.astype(jnp.bfloat16) if step < levels - 1 else child
    local = (leaf_local + current).astype(jnp.bfloat16)
    far = jnp.einsum('kba,kcb->cba', harm_box.astype(jnp.float32), local.astype(jnp.float32)).reshape(C, ATOMS)

    flat_masked = masked.reshape(C, ATOMS)
    padded = jnp.pad(flat_masked, ((0, 0), (GHOST, GHOST)))

    def near_block(block):
        start = (block * ATOM_DEV).astype(jnp.int32)
        index_rows = lax.dynamic_slice_in_dim(neighbours, start, ATOM_DEV, 1)
        weight_rows = lax.dynamic_slice_in_dim(edge_weights, start, ATOM_DEV, 1)
        window = lax.dynamic_slice_in_dim(padded, start, ATOM_DEV + 2 * GHOST, 1)
        got = window[:, index_rows]
        return jnp.einsum('csa,sa->ca', got.astype(jnp.float32), weight_rows.astype(jnp.float32))

    near = lax.map(near_block, jnp.arange(TOPS, dtype=jnp.int32))
    near = near.transpose(1, 0, 2).reshape(C, ATOMS)
    return (far + near).astype(jnp.bfloat16)
```

```python
import jax
import jax.numpy as jnp
from jax import lax
from jax.experimental import pallas as pl
from jax.experimental.pallas import tpu as pltpu
from jax.sharding import PartitionSpec as P

VBLK = 27


def padded(shard, sides, width):
    for axis, dim in sides:
        devices, length = (lax.axis_size(axis), shard.shape[dim])
        up = [(i, (i + 1) % devices) for i in range(devices - 1)]
        down = [(j, i) for i, j in up]
        last = lax.slice_in_dim(shard, length - width, length, axis=dim)
        initial = lax.slice_in_dim(shard, 0, width, axis=dim)
        before = lax.ppermute(last, axis, up)
        after = lax.ppermute(initial, axis, down)
        shard = jnp.concatenate([before, shard, after], axis=dim)
    return shard


HI = 256
TILE = 256


def near_kernel(table_ref, index_ref, weight_ref, out_ref, weight_f32):
    slots, tile = index_ref.shape
    rows, high = table_ref.shape
    chans = out_ref.shape[0]
    groups = rows // chans
    weight_f32[...] = weight_ref[...].astype(jnp.float32)
    lane_rows = lax.broadcasted_iota(jnp.int32, (high, tile), 0).astype(jnp.bfloat16)
    group_rows = lax.broadcasted_iota(jnp.int32, (groups, tile), 0)

    def step(slot, total):
        index = index_ref[pl.ds(slot, 1), :]
        weight = weight_f32[pl.ds(slot, 1), :]
        low = (index & (high - 1)).astype(jnp.float32).astype(jnp.bfloat16)
        hot = jnp.where(lane_rows == low, jnp.bfloat16(1), jnp.bfloat16(0))
        got = jnp.dot(table_ref[...], hot, preferred_element_type=jnp.float32)
        group = lax.shift_right_logical(index, 8)
        scale = jnp.where(group_rows == group, weight, 0.0)
        terms = got.reshape(chans, groups // 8, 8, tile) * scale.reshape(1, groups // 8, 8, tile)
        return total + jnp.sum(terms, axis=1)

    total = lax.fori_loop(0, slots, step, jnp.zeros((chans, 8, tile), jnp.float32), unroll=2)
    out_ref[...] = jnp.sum(total, axis=1)


def near_field(ext_charges, neighbours, edge_weights):
    chans, window = ext_charges.shape
    slots, atoms = neighbours.shape
    table = ext_charges.reshape(chans * (window // HI), HI)
    return pl.pallas_call(
        near_kernel,
        grid=(atoms // TILE,),
        in_specs=[
            pl.BlockSpec(table.shape, lambda i: (0, 0)),
            pl.BlockSpec((slots, TILE), lambda i: (0, i)),
            pl.BlockSpec((slots, TILE), lambda i: (0, i)),
        ],
        out_specs=pl.BlockSpec((chans, TILE), lambda i: (0, i)),
        out_shape=jax.ShapeDtypeStruct((chans, atoms), jnp.float32),
        scratch_shapes=[pltpu.VMEM((slots, TILE), jnp.float32)],
        compiler_params=pltpu.CompilerParams(vmem_limit_bytes=48 * 1024 * 1024),
        cost_estimate=pl.CostEstimate(
            flops=2 * slots * atoms * chans * window, bytes_accessed=slots * atoms * 6, transcendentals=0
        ),
        name="near_field",
    )(table, neighbours, edge_weights)


def body(
    charges,
    harmonics,
    counts,
    m2l_ops,
    m2m_ops,
    l2l_ops,
    sources,
    list_mask,
    top_sources,
    top_vectors,
    neighbours,
    edge_weights,
):
    ncoef = harmonics.shape[0]
    chans = charges.shape[0]
    box_dev = counts.shape[0]
    atom_dev = charges.shape[1]
    slots = atom_dev // box_dev
    ghost = atom_dev // 4
    nvec = sources.shape[0]
    position = lax.axis_index("box")
    live = jnp.arange(slots, dtype=jnp.int32)[None, :] < counts[:, None]
    masked = jnp.where(
        live[None], charges.reshape(chans, box_dev, slots), jnp.zeros((), jnp.bfloat16)
    )
    flat_masked = masked.reshape(chans, atom_dev)
    harm_box = harmonics.reshape(ncoef, box_dev, slots)
    mult = jnp.einsum("kba,cba->kcb", harm_box, masked, preferred_element_type=jnp.float32).astype(
        jnp.bfloat16
    )
    edge_size = chans * ghost
    mult_size = ncoef * chans * box_dev
    reach = edge_size + mult_size
    low_edge = flat_masked[:, :ghost].reshape(edge_size)
    high_edge = flat_masked[:, atom_dev - ghost :].reshape(edge_size)
    packed = jnp.concatenate([low_edge, mult.reshape(mult_size), high_edge])
    extended = padded(packed, (("box", 0),), reach)
    from_low = extended[:reach]
    from_high = extended[extended.shape[0] - reach :]
    mult_low = from_low[:mult_size].reshape(ncoef, chans, box_dev)
    charge_low = from_low[mult_size:].reshape(chans, ghost)
    charge_high = from_high[:edge_size].reshape(chans, ghost)
    mult_high = from_high[edge_size:].reshape(ncoef, chans, box_dev)
    ext_charges = jnp.concatenate([charge_low, flat_masked, charge_high], axis=1)
    ext_mult = jnp.concatenate([mult_low, mult, mult_high], axis=2)
    level = mult
    while level.shape[2] > 1:
        grouped = level.reshape(ncoef, chans, level.shape[2] // 8, 8)
        level = jnp.einsum(
            "okl,lcpo->kcp", m2m_ops, grouped, preferred_element_type=jnp.float32
        ).astype(jnp.bfloat16)
    operators = m2l_ops.reshape(ncoef, nvec, ncoef)
    row_sources = lax.dynamic_slice_in_dim(top_sources, position, 1, 0)[0]
    row_vectors = lax.dynamic_slice_in_dim(top_vectors, position, 1, 0)[0]
    piece = lax.all_gather(level, "box", axis=2, tiled=True)
    columns = jnp.arange(piece.shape[2], dtype=jnp.int32)
    hits = (row_sources[:, None] == columns[None, :]).astype(jnp.bfloat16)
    picked = jnp.einsum("jn,kcn->jkc", hits, piece, preferred_element_type=jnp.float32)
    chosen = jnp.take(operators, row_vectors, axis=1)
    top_local = jnp.einsum(
        "kjl,jlc->kc", chosen, picked.astype(jnp.bfloat16), preferred_element_type=jnp.float32
    )
    current = top_local.astype(jnp.bfloat16).reshape(ncoef, chans, 1)
    local_index = sources - (position - 1) * box_dev
    leaf_local = jnp.zeros((ncoef, chans * box_dev), jnp.float32)
    for offset in range(0, nvec, VBLK):
        index_block = local_index[offset : offset + VBLK]
        mask_block = list_mask[offset : offset + VBLK].astype(jnp.bfloat16)
        picked_block = ext_mult[:, :, index_block] * mask_block[None, None]
        stacked = picked_block.transpose(2, 0, 1, 3).reshape(VBLK * ncoef, chans * box_dev)
        ops_block = m2l_ops[:, offset * ncoef : (offset + VBLK) * ncoef]
        leaf_local = leaf_local + jnp.dot(ops_block, stacked, preferred_element_type=jnp.float32)
    leaf_local = leaf_local.reshape(ncoef, chans, box_dev)
    levels = 0
    width = 1
    while width < box_dev:
        width = width * 8
        levels = levels + 1
    child = jnp.einsum("okl,lcp->kcpo", l2l_ops, current, preferred_element_type=jnp.float32)
    child = child.reshape(ncoef, chans, current.shape[2] * 8)
    local = (leaf_local + child).astype(jnp.bfloat16)
    far = jnp.einsum("kba,kcb->cba", harm_box, local, preferred_element_type=jnp.float32).reshape(
        chans, atom_dev
    )
    near = near_field(ext_charges, neighbours, edge_weights)
    return (far + near).astype(jnp.bfloat16)


def solution(mesh):
    return jax.shard_map(
        body,
        mesh=mesh,
        in_specs=(
            P(None, ("sys", "box")),
            P(None, ("sys", "box")),
            P(("sys", "box")),
            P(),
            P(),
            P(),
            P(None, ("sys", "box")),
            P(None, ("sys", "box")),
            P("sys", None),
            P("sys", None),
            P(None, ("sys", "box")),
            P(None, ("sys", "box")),
        ),
        out_specs=P(None, ("sys", "box")),
        check_vma=False,
    )
```

```python
import jax
import jax.numpy as jnp
from jax import lax
from jax.experimental import pallas as pl
from jax.experimental.pallas import tpu as pltpu
from jax.sharding import PartitionSpec as P


HI = 256
TILE = 256


def near_kernel(table_ref, index_ref, weight_ref, out_ref, weight_f32):
    slots, tile = index_ref.shape
    rows, high = table_ref.shape
    chans = out_ref.shape[0]
    groups = rows // chans
    weight_f32[...] = weight_ref[...].astype(jnp.float32)
    lane_rows = lax.broadcasted_iota(jnp.int32, (high, tile), 0).astype(jnp.bfloat16)
    group_rows = lax.broadcasted_iota(jnp.int32, (groups, tile), 0)

    def step(slot, total):
        index = index_ref[pl.ds(slot, 1), :]
        weight = weight_f32[pl.ds(slot, 1), :]
        low = (index & (high - 1)).astype(jnp.float32).astype(jnp.bfloat16)
        hot = jnp.where(lane_rows == low, jnp.bfloat16(1), jnp.bfloat16(0))
        got = jnp.dot(table_ref[...], hot, preferred_element_type=jnp.float32)
        group = lax.shift_right_logical(index, 8)
        scale = jnp.where(group_rows == group, weight, 0.0)
        terms = got.reshape(chans, groups // 8, 8, tile) * scale.reshape(1, groups // 8, 8, tile)
        return total + jnp.sum(terms, axis=1)

    total = lax.fori_loop(0, slots, step, jnp.zeros((chans, 8, tile), jnp.float32), unroll=2)
    out_ref[...] = jnp.sum(total, axis=1)


def near_field(ext_charges, neighbours, edge_weights):
    chans, window = ext_charges.shape
    slots, atoms = neighbours.shape
    table = ext_charges.reshape(chans * (window // HI), HI)
    return pl.pallas_call(
        near_kernel,
        grid=(atoms // TILE,),
        in_specs=[
            pl.BlockSpec(table.shape, lambda i: (0, 0)),
            pl.BlockSpec((slots, TILE), lambda i: (0, i)),
            pl.BlockSpec((slots, TILE), lambda i: (0, i)),
        ],
        out_specs=pl.BlockSpec((chans, TILE), lambda i: (0, i)),
        out_shape=jax.ShapeDtypeStruct((chans, atoms), jnp.float32),
        scratch_shapes=[pltpu.VMEM((slots, TILE), jnp.float32)],
        compiler_params=pltpu.CompilerParams(vmem_limit_bytes=48 * 1024 * 1024),
        cost_estimate=pl.CostEstimate(
            flops=2 * slots * atoms * chans * window, bytes_accessed=slots * atoms * 6, transcendentals=0
        ),
        name="near_field",
    )(table, neighbours, edge_weights)


CHUNK = 2048


def field_kernel(
    source_ref,
    top_source_ref,
    top_vector_ref,
    table_ref,
    tops_ref,
    ops_ref,
    l2l_ref,
    harmonics_ref,
    near_ref,
    out_ref,
    table,
    tops,
    stack,
):
    ncoef, columns = ops_ref.shape
    chans, atoms = out_ref.shape
    nvec = columns // ncoef
    boxes = source_ref.shape[0] // nvec
    leaf_rows = boxes * chans
    slots = atoms // boxes
    table[:, :ncoef] = table_ref[...].astype(jnp.float32)
    tops[...] = jnp.zeros_like(tops)
    tops[:, :ncoef] = tops_ref[...].astype(jnp.float32)
    for vec in range(nvec):
        for box in range(boxes):
            row = pl.multiple_of(source_ref[vec * boxes + box] * chans, chans)
            stack[box * chans : (box + 1) * chans, vec * ncoef : (vec + 1) * ncoef] = table[
                pl.ds(row, chans), :ncoef
            ]
    stack[leaf_rows:, :] = jnp.zeros((chans, stack.shape[1]), jnp.float32)

    def add_entry(entry, carry):
        row = pl.multiple_of(top_source_ref[entry] * chans, chans)
        column = top_vector_ref[entry] * ncoef
        shift = column & 127
        start = pl.multiple_of(column - shift, 128)
        wide = jnp.concatenate(
            [tops[pl.ds(row, chans), :], jnp.zeros((chans, 128), jnp.float32)], axis=1
        )
        moved = pltpu.roll(wide, shift, 1)
        stack[leaf_rows:, pl.ds(start, 256)] = stack[leaf_rows:, pl.ds(start, 256)] + moved
        return carry

    lax.fori_loop(0, top_source_ref.shape[0], add_entry, 0)
    total = jnp.zeros((leaf_rows + chans, ncoef), jnp.float32)
    for start in range(0, columns, CHUNK):
        stop = min(start + CHUNK, columns)
        total = total + lax.dot_general(
            stack[:, start:stop].astype(jnp.bfloat16),
            ops_ref[:, start:stop],
            (((1,), (1,)), ((), ())),
            preferred_element_type=jnp.float32,
        )
    parent = total[leaf_rows:].astype(jnp.bfloat16)
    for box in range(boxes):
        child = lax.dot_general(
            parent,
            l2l_ref[box],
            (((1,), (1,)), ((), ())),
            preferred_element_type=jnp.float32,
        )
        local = (total[box * chans : (box + 1) * chans] + child).astype(jnp.bfloat16)
        span = slice(box * slots, (box + 1) * slots)
        far = jnp.dot(local, harmonics_ref[:, span], preferred_element_type=jnp.float32)
        out_ref[:, span] = (far + near_ref[:, span]).astype(out_ref.dtype)


def field(source, top_source, top_vector, table, tops, ops, l2l_ops, harmonics, near):
    chans, atoms = near.shape
    ncoef, columns = ops.shape
    boxes = l2l_ops.shape[0]
    rows = (boxes + 1) * chans
    width = (columns // 128 + 2) * 128
    smem = pl.BlockSpec(memory_space=pltpu.SMEM)
    vmem = pl.BlockSpec(memory_space=pltpu.VMEM)
    return pl.pallas_call(
        field_kernel,
        in_specs=[smem] * 3 + [vmem] * 6,
        out_specs=vmem,
        out_shape=jax.ShapeDtypeStruct((chans, atoms), jnp.bfloat16),
        scratch_shapes=[
            pltpu.VMEM((table.shape[0], 128), jnp.float32),
            pltpu.VMEM((tops.shape[0], 128), jnp.float32),
            pltpu.VMEM((rows, width), jnp.float32),
        ],
        compiler_params=pltpu.CompilerParams(vmem_limit_bytes=56 * 1024 * 1024),
        cost_estimate=pl.CostEstimate(
            flops=2 * rows * ncoef * columns, bytes_accessed=2 * ncoef * (columns + atoms), transcendentals=0
        ),
        name="field",
    )(source, top_source, top_vector, table, tops, ops, l2l_ops, harmonics, near)


def body(
    charges,
    harmonics,
    counts,
    m2l_ops,
    m2m_ops,
    l2l_ops,
    sources,
    list_mask,
    top_sources,
    top_vectors,
    neighbours,
    edge_weights,
):
    ncoef = harmonics.shape[0]
    chans = charges.shape[0]
    box_dev = counts.shape[0]
    atom_dev = charges.shape[1]
    slots = atom_dev // box_dev
    ghost = atom_dev // 4
    position = lax.axis_index("box")
    live = jnp.arange(slots, dtype=jnp.int32)[None, :] < counts[:, None]
    masked = jnp.where(
        live[None], charges.reshape(chans, box_dev, slots), jnp.zeros((), jnp.bfloat16)
    )
    flat_masked = masked.reshape(chans, atom_dev)
    harm_box = harmonics.reshape(ncoef, box_dev, slots)
    mult = jnp.einsum("cba,kba->bck", masked, harm_box, preferred_element_type=jnp.float32).astype(
        jnp.bfloat16
    )
    top = jnp.einsum("ocl,okl->ck", mult, m2m_ops, preferred_element_type=jnp.float32).astype(
        jnp.bfloat16
    )
    tops = lax.all_gather(top, "box", axis=0, tiled=True)
    devices = lax.axis_size("box")
    up = [(i, (i + 1) % devices) for i in range(devices - 1)]
    down = [(j, i) for i, j in up]
    charge_low = lax.ppermute(flat_masked[:, atom_dev - ghost :], "box", up)
    charge_high = lax.ppermute(flat_masked[:, :ghost], "box", down)
    rows = mult.reshape(box_dev * chans, ncoef)
    rows_low = lax.ppermute(rows, "box", up)
    rows_high = lax.ppermute(rows, "box", down)
    ext_charges = jnp.concatenate([charge_low, flat_masked, charge_high], axis=1)
    near = near_field(ext_charges, neighbours, edge_weights)
    table = jnp.concatenate(
        [rows_low, rows, rows_high, jnp.zeros((chans, ncoef), jnp.bfloat16)], axis=0
    )
    local_index = sources - (position - 1) * box_dev
    local_index = jnp.where(list_mask != 0, local_index, 3 * box_dev).reshape(-1)
    row_sources = lax.dynamic_slice_in_dim(top_sources, position, 1, 0)[0]
    row_vectors = lax.dynamic_slice_in_dim(top_vectors, position, 1, 0)[0]
    return field(
        local_index, row_sources, row_vectors, table, tops, m2l_ops, l2l_ops, harmonics, near
    )


def solution(mesh):
    return jax.shard_map(
        body,
        mesh=mesh,
        in_specs=(
            P(None, ("sys", "box")),
            P(None, ("sys", "box")),
            P(("sys", "box")),
            P(),
            P(),
            P(),
            P(None, ("sys", "box")),
            P(None, ("sys", "box")),
            P("sys", None),
            P("sys", None),
            P(None, ("sys", "box")),
            P(None, ("sys", "box")),
        ),
        out_specs=P(None, ("sys", "box")),
        check_vma=False,
    )
```

```python
import jax
import jax.numpy as jnp
from jax import lax
from jax.experimental import pallas as pl
from jax.experimental.pallas import tpu as pltpu
from jax.sharding import PartitionSpec as P


HI = 256
TILE = 256


def near_kernel(table_ref, index_ref, weight_ref, out_ref, weight_f32):
    slots, tile = index_ref.shape
    rows, high = table_ref.shape
    chans = out_ref.shape[0]
    groups = rows // chans
    weight_f32[...] = weight_ref[...].astype(jnp.float32)
    lane_rows = lax.broadcasted_iota(jnp.int32, (high, tile), 0).astype(jnp.bfloat16)
    group_rows = lax.broadcasted_iota(jnp.int32, (groups, tile), 0)

    def step(slot, total):
        index = index_ref[pl.ds(slot, 1), :]
        weight = weight_f32[pl.ds(slot, 1), :]
        low = (index & (high - 1)).astype(jnp.float32).astype(jnp.bfloat16)
        hot = jnp.where(lane_rows == low, jnp.bfloat16(1), jnp.bfloat16(0))
        got = jnp.dot(table_ref[...], hot, preferred_element_type=jnp.float32)
        group = lax.shift_right_logical(index, 8)
        scale = jnp.where(group_rows == group, weight, 0.0)
        terms = got.reshape(chans, groups // 8, 8, tile) * scale.reshape(1, groups // 8, 8, tile)
        return total + jnp.sum(terms, axis=1)

    total = lax.fori_loop(0, slots, step, jnp.zeros((chans, 8, tile), jnp.float32), unroll=2)
    out_ref[...] = jnp.sum(total, axis=1)


def near_field(ext_charges, neighbours, edge_weights):
    chans, window = ext_charges.shape
    slots, atoms = neighbours.shape
    table = ext_charges.reshape(chans * (window // HI), HI)
    return pl.pallas_call(
        near_kernel,
        grid=(atoms // TILE,),
        in_specs=[
            pl.BlockSpec(table.shape, lambda i: (0, 0)),
            pl.BlockSpec((slots, TILE), lambda i: (0, i)),
            pl.BlockSpec((slots, TILE), lambda i: (0, i)),
        ],
        out_specs=pl.BlockSpec((chans, TILE), lambda i: (0, i)),
        out_shape=jax.ShapeDtypeStruct((chans, atoms), jnp.float32),
        scratch_shapes=[pltpu.VMEM((slots, TILE), jnp.float32)],
        compiler_params=pltpu.CompilerParams(vmem_limit_bytes=48 * 1024 * 1024),
        cost_estimate=pl.CostEstimate(
            flops=2 * slots * atoms * chans * window, bytes_accessed=slots * atoms * 6, transcendentals=0
        ),
        name="near_field",
    )(table, neighbours, edge_weights)


def exchange_kernel(
    top_ref,
    rows_ref,
    first_ref,
    last_ref,
    tops_ref,
    rows_low_ref,
    rows_high_ref,
    charge_low_ref,
    charge_high_ref,
    top_send,
    top_recv,
    edge_send,
    edge_recv,
):
    devices = lax.axis_size("box")
    me = lax.axis_index("box")
    part = lax.axis_index("sys")
    chans = top_ref.shape[0]
    mesh_ids = pl.DeviceIdType.MESH
    barrier = pltpu.get_barrier_semaphore()

    def greet(step, carry):
        peer = lax.rem(me + step, devices)
        pl.semaphore_signal(barrier, inc=1, device_id=(part, peer), device_id_type=mesh_ids)
        return carry

    lax.fori_loop(1, devices, greet, 0)
    pl.semaphore_wait(barrier, devices - 1)

    right = lax.rem(me + 1, devices)
    left = lax.rem(me + devices - 1, devices)
    edges = []
    for spot, (source, target, peer) in enumerate(
        (
            (rows_ref, rows_low_ref, right),
            (rows_ref, rows_high_ref, left),
            (last_ref, charge_low_ref, right),
            (first_ref, charge_high_ref, left),
        )
    ):
        edges.append(
            pltpu.make_async_remote_copy(
                src_ref=source,
                dst_ref=target,
                send_sem=edge_send.at[spot],
                recv_sem=edge_recv.at[spot],
                device_id=(part, peer),
                device_id_type=mesh_ids,
            )
        )

    def top_copy(step):
        peer = lax.rem(me + step, devices)
        return pltpu.make_async_remote_copy(
            src_ref=top_ref,
            dst_ref=tops_ref.at[pl.ds(pl.multiple_of(me * chans, chans), chans)],
            send_sem=top_send.at[step],
            recv_sem=top_recv.at[step],
            device_id=(part, peer),
            device_id_type=mesh_ids,
        )

    def send(step, carry):
        top_copy(step).start()
        return carry

    def receive(step, carry):
        origin = lax.rem(me + devices - step, devices)
        pltpu.make_async_remote_copy(
            src_ref=top_ref,
            dst_ref=tops_ref.at[pl.ds(pl.multiple_of(origin * chans, chans), chans)],
            send_sem=top_send.at[step],
            recv_sem=top_recv.at[step],
            device_id=(part, lax.rem(me + step, devices)),
            device_id_type=mesh_ids,
        ).wait()
        return carry

    for copy in edges:
        copy.start()
    lax.fori_loop(1, devices, send, 0)
    tops_ref[pl.ds(pl.multiple_of(me * chans, chans), chans), :] = top_ref[...]
    for copy in edges:
        copy.wait()
    lax.fori_loop(1, devices, receive, 0)


def exchange(top, rows, first, last):
    devices = lax.axis_size("box")
    chans, width = top.shape
    vmem = pl.BlockSpec(memory_space=pltpu.VMEM)
    return pl.pallas_call(
        exchange_kernel,
        in_specs=[vmem] * 4,
        out_specs=[vmem] * 5,
        out_shape=[
            jax.ShapeDtypeStruct((devices * chans, width), jnp.bfloat16),
            jax.ShapeDtypeStruct(rows.shape, jnp.bfloat16),
            jax.ShapeDtypeStruct(rows.shape, jnp.bfloat16),
            jax.ShapeDtypeStruct(last.shape, jnp.bfloat16),
            jax.ShapeDtypeStruct(first.shape, jnp.bfloat16),
        ],
        scratch_shapes=[
            pltpu.SemaphoreType.DMA((devices,)),
            pltpu.SemaphoreType.DMA((devices,)),
            pltpu.SemaphoreType.DMA((4,)),
            pltpu.SemaphoreType.DMA((4,)),
        ],
        compiler_params=pltpu.CompilerParams(collective_id=0, has_side_effects=True),
        name="exchange",
    )(top, rows, first, last)


CHUNK = 2048


def field_kernel(
    source_ref,
    top_source_ref,
    top_vector_ref,
    table_ref,
    tops_ref,
    ops_ref,
    l2l_ref,
    harmonics_ref,
    near_ref,
    out_ref,
    table,
    tops,
    stack,
):
    columns, ncoef = ops_ref.shape
    chans, atoms = out_ref.shape
    nvec = columns // ncoef
    boxes = source_ref.shape[0] // nvec
    leaf_rows = boxes * chans
    slots = atoms // boxes
    table[...] = table_ref[...].astype(jnp.float32)
    tops[...] = tops_ref[...].astype(jnp.float32)
    for vec in range(nvec):
        for box in range(boxes):
            row = pl.multiple_of(source_ref[vec * boxes + box] * chans, chans)
            stack[box * chans : (box + 1) * chans, vec * ncoef : (vec + 1) * ncoef] = table[
                pl.ds(row, chans), :ncoef
            ]
    stack[leaf_rows:, :] = jnp.zeros((chans, stack.shape[1]), jnp.float32)

    def add_entry(entry, carry):
        row = pl.multiple_of(top_source_ref[entry] * chans, chans)
        column = top_vector_ref[entry] * ncoef
        shift = column & 127
        start = pl.multiple_of(column - shift, 128)
        wide = jnp.concatenate(
            [tops[pl.ds(row, chans), :], jnp.zeros((chans, 128), jnp.float32)], axis=1
        )
        moved = pltpu.roll(wide, shift, 1)
        stack[leaf_rows:, pl.ds(start, 256)] = stack[leaf_rows:, pl.ds(start, 256)] + moved
        return carry

    lax.fori_loop(0, top_source_ref.shape[0], add_entry, 0)
    total = jnp.zeros((leaf_rows + 2 * chans, ncoef), jnp.float32)
    for start in range(0, columns, CHUNK):
        stop = min(start + CHUNK, columns)
        values = stack[:, start:stop]
        high = values.astype(jnp.bfloat16)
        rest = (values[leaf_rows:] - high[leaf_rows:].astype(jnp.float32)).astype(jnp.bfloat16)
        total = total + jnp.dot(
            jnp.concatenate([high, rest], axis=0),
            ops_ref[start:stop, :],
            preferred_element_type=jnp.float32,
        )
    parent = (total[leaf_rows : leaf_rows + chans] + total[leaf_rows + chans :]).astype(jnp.bfloat16)
    for box in range(boxes):
        child = lax.dot_general(
            parent,
            l2l_ref[box],
            (((1,), (1,)), ((), ())),
            preferred_element_type=jnp.float32,
        )
        local = (total[box * chans : (box + 1) * chans] + child).astype(jnp.bfloat16)
        span = slice(box * slots, (box + 1) * slots)
        far = jnp.dot(local, harmonics_ref[:, span], preferred_element_type=jnp.float32)
        out_ref[:, span] = (far + near_ref[:, span]).astype(out_ref.dtype)


def field(source, top_source, top_vector, table, tops, ops, l2l_ops, harmonics, near):
    chans, atoms = near.shape
    columns, ncoef = ops.shape
    boxes = l2l_ops.shape[0]
    rows = (boxes + 1) * chans
    width = (columns // 128 + 2) * 128
    smem = pl.BlockSpec(memory_space=pltpu.SMEM)
    vmem = pl.BlockSpec(memory_space=pltpu.VMEM)
    return pl.pallas_call(
        field_kernel,
        in_specs=[smem] * 3 + [vmem] * 6,
        out_specs=vmem,
        out_shape=jax.ShapeDtypeStruct((chans, atoms), jnp.bfloat16),
        scratch_shapes=[
            pltpu.VMEM((table.shape[0], 128), jnp.float32),
            pltpu.VMEM((tops.shape[0], 128), jnp.float32),
            pltpu.VMEM((rows, width), jnp.float32),
        ],
        compiler_params=pltpu.CompilerParams(vmem_limit_bytes=56 * 1024 * 1024),
        cost_estimate=pl.CostEstimate(
            flops=2 * rows * ncoef * columns, bytes_accessed=2 * ncoef * (columns + atoms), transcendentals=0
        ),
        name="field",
    )(source, top_source, top_vector, table, tops, ops, l2l_ops, harmonics, near)


def body(
    charges,
    harmonics,
    counts,
    m2l_ops,
    m2m_ops,
    l2l_ops,
    sources,
    list_mask,
    top_sources,
    top_vectors,
    neighbours,
    edge_weights,
):
    ncoef = harmonics.shape[0]
    chans = charges.shape[0]
    box_dev = counts.shape[0]
    atom_dev = charges.shape[1]
    slots = atom_dev // box_dev
    ghost = atom_dev // 4
    position = lax.axis_index("box")
    live = jnp.arange(slots, dtype=jnp.int32)[None, :] < counts[:, None]
    masked = jnp.where(
        live[None], charges.reshape(chans, box_dev, slots), jnp.zeros((), jnp.bfloat16)
    )
    flat_masked = masked.reshape(chans, atom_dev)
    harm_box = harmonics.reshape(ncoef, box_dev, slots)
    mult = jnp.einsum("cba,kba->bck", masked, harm_box, preferred_element_type=jnp.float32).astype(
        jnp.bfloat16
    )
    top = jnp.einsum("ocl,okl->ck", mult, m2m_ops, preferred_element_type=jnp.float32).astype(
        jnp.bfloat16
    )
    rows = mult.reshape(box_dev * chans, ncoef)
    rows = jnp.pad(rows, ((0, 0), (0, 128 - ncoef)))
    top = jnp.pad(top, ((0, 0), (0, 128 - ncoef)))
    tops, rows_low, rows_high, charge_low, charge_high = exchange(
        top, rows, flat_masked[:, :ghost], flat_masked[:, atom_dev - ghost :]
    )
    last = lax.axis_size("box") - 1
    charge_low = jnp.where(position == 0, jnp.zeros((), jnp.bfloat16), charge_low)
    charge_high = jnp.where(position == last, jnp.zeros((), jnp.bfloat16), charge_high)
    ext_charges = jnp.concatenate([charge_low, flat_masked, charge_high], axis=1)
    near = near_field(ext_charges, neighbours, edge_weights)
    table = jnp.concatenate(
        [rows_low, rows, rows_high, jnp.zeros((chans, 128), jnp.bfloat16)], axis=0
    )
    local_index = sources - (position - 1) * box_dev
    local_index = jnp.where(list_mask != 0, local_index, 3 * box_dev).reshape(-1)
    row_sources = lax.dynamic_slice_in_dim(top_sources, position, 1, 0)[0]
    row_vectors = lax.dynamic_slice_in_dim(top_vectors, position, 1, 0)[0]
    return field(
        local_index, row_sources, row_vectors, table, tops, m2l_ops.T, l2l_ops, harmonics, near
    )


def solution(mesh):
    return jax.shard_map(
        body,
        mesh=mesh,
        in_specs=(
            P(None, ("sys", "box")),
            P(None, ("sys", "box")),
            P(("sys", "box")),
            P(),
            P(),
            P(),
            P(None, ("sys", "box")),
            P(None, ("sys", "box")),
            P("sys", None),
            P("sys", None),
            P(None, ("sys", "box")),
            P(None, ("sys", "box")),
        ),
        out_specs=P(None, ("sys", "box")),
        check_vma=False,
    )
```

```python
import jax
import jax.numpy as jnp
from jax import lax
from jax.experimental import pallas as pl
from jax.experimental.pallas import tpu as pltpu
from jax.sharding import PartitionSpec as P


HI = 256
TILE = 512


def near_kernel(table_ref, index_ref, weight_ref, out_ref, weight_f32):
    slots, tile = index_ref.shape
    rows, high = table_ref.shape
    chans = out_ref.shape[0]
    groups = rows // chans
    weight_f32[...] = weight_ref[...].astype(jnp.float32)
    lane_rows = lax.broadcasted_iota(jnp.int32, (high, tile), 0).astype(jnp.bfloat16)
    group_rows = lax.broadcasted_iota(jnp.int32, (groups, tile), 0)

    def step(slot, total):
        index = index_ref[pl.ds(slot, 1), :]
        weight = weight_f32[pl.ds(slot, 1), :]
        low = (index & (high - 1)).astype(jnp.float32).astype(jnp.bfloat16)
        hot = jnp.where(lane_rows == low, jnp.bfloat16(1), jnp.bfloat16(0))
        got = jnp.dot(table_ref[...], hot, preferred_element_type=jnp.float32)
        group = lax.shift_right_logical(index, 8)
        scale = jnp.where(group_rows == group, weight, 0.0)
        terms = got.reshape(chans, groups // 8, 8, tile) * scale.reshape(1, groups // 8, 8, tile)
        return total + jnp.sum(terms, axis=1)

    total = lax.fori_loop(0, slots, step, jnp.zeros((chans, 8, tile), jnp.float32), unroll=True)
    out_ref[...] = jnp.sum(total, axis=1)


def near_field(ext_charges, neighbours, edge_weights):
    chans, window = ext_charges.shape
    slots, atoms = neighbours.shape
    table = ext_charges.reshape(chans * (window // HI), HI)
    return pl.pallas_call(
        near_kernel,
        grid=(atoms // TILE,),
        in_specs=[
            pl.BlockSpec(table.shape, lambda i: (0, 0)),
            pl.BlockSpec((slots, TILE), lambda i: (0, i)),
            pl.BlockSpec((slots, TILE), lambda i: (0, i)),
        ],
        out_specs=pl.BlockSpec((chans, TILE), lambda i: (0, i)),
        out_shape=jax.ShapeDtypeStruct((chans, atoms), jnp.float32),
        scratch_shapes=[pltpu.VMEM((slots, TILE), jnp.float32)],
        compiler_params=pltpu.CompilerParams(vmem_limit_bytes=48 * 1024 * 1024),
        cost_estimate=pl.CostEstimate(
            flops=2 * slots * atoms * chans * window, bytes_accessed=slots * atoms * 6, transcendentals=0
        ),
        name="near_field",
    )(table, neighbours, edge_weights)


def exchange_kernel(
    top_ref,
    rows_ref,
    first_ref,
    last_ref,
    tops_ref,
    rows_low_ref,
    rows_high_ref,
    charge_low_ref,
    charge_high_ref,
    top_send,
    top_recv,
    edge_send,
    edge_recv,
):
    devices = lax.axis_size("box")
    me = lax.axis_index("box")
    part = lax.axis_index("sys")
    chans = top_ref.shape[0]
    mesh_ids = pl.DeviceIdType.MESH
    barrier = pltpu.get_barrier_semaphore()

    def greet(step, carry):
        peer = lax.rem(me + step, devices)
        pl.semaphore_signal(barrier, inc=1, device_id=(part, peer), device_id_type=mesh_ids)
        return carry

    lax.fori_loop(1, devices, greet, 0)
    pl.semaphore_wait(barrier, devices - 1)

    right = lax.rem(me + 1, devices)
    left = lax.rem(me + devices - 1, devices)
    edges = []
    for spot, (source, target, peer) in enumerate(
        (
            (rows_ref, rows_low_ref, right),
            (rows_ref, rows_high_ref, left),
            (last_ref, charge_low_ref, right),
            (first_ref, charge_high_ref, left),
        )
    ):
        edges.append(
            pltpu.make_async_remote_copy(
                src_ref=source,
                dst_ref=target,
                send_sem=edge_send.at[spot],
                recv_sem=edge_recv.at[spot],
                device_id=(part, peer),
                device_id_type=mesh_ids,
            )
        )

    def top_copy(step):
        peer = lax.rem(me + step, devices)
        return pltpu.make_async_remote_copy(
            src_ref=top_ref,
            dst_ref=tops_ref.at[pl.ds(pl.multiple_of(me * chans, chans), chans)],
            send_sem=top_send.at[step],
            recv_sem=top_recv.at[step],
            device_id=(part, peer),
            device_id_type=mesh_ids,
        )

    def send(step, carry):
        top_copy(step).start()
        return carry

    def receive(step, carry):
        origin = lax.rem(me + devices - step, devices)
        pltpu.make_async_remote_copy(
            src_ref=top_ref,
            dst_ref=tops_ref.at[pl.ds(pl.multiple_of(origin * chans, chans), chans)],
            send_sem=top_send.at[step],
            recv_sem=top_recv.at[step],
            device_id=(part, lax.rem(me + step, devices)),
            device_id_type=mesh_ids,
        ).wait()
        return carry

    for copy in edges:
        copy.start()
    lax.fori_loop(1, devices, send, 0)
    tops_ref[pl.ds(pl.multiple_of(me * chans, chans), chans), :] = top_ref[...]
    for copy in edges:
        copy.wait()
    lax.fori_loop(1, devices, receive, 0)


def exchange(top, rows, first, last):
    devices = lax.axis_size("box")
    chans, width = top.shape
    vmem = pl.BlockSpec(memory_space=pltpu.VMEM)
    return pl.pallas_call(
        exchange_kernel,
        in_specs=[vmem] * 4,
        out_specs=[vmem] * 5,
        out_shape=[
            jax.ShapeDtypeStruct((devices * chans, width), jnp.bfloat16),
            jax.ShapeDtypeStruct(rows.shape, jnp.bfloat16),
            jax.ShapeDtypeStruct(rows.shape, jnp.bfloat16),
            jax.ShapeDtypeStruct(last.shape, jnp.bfloat16),
            jax.ShapeDtypeStruct(first.shape, jnp.bfloat16),
        ],
        scratch_shapes=[
            pltpu.SemaphoreType.DMA((devices,)),
            pltpu.SemaphoreType.DMA((devices,)),
            pltpu.SemaphoreType.DMA((4,)),
            pltpu.SemaphoreType.DMA((4,)),
        ],
        compiler_params=pltpu.CompilerParams(collective_id=0, has_side_effects=True),
        name="exchange",
    )(top, rows, first, last)


CHUNK = 2048


def field_kernel(
    source_ref,
    top_source_ref,
    top_vector_ref,
    table_ref,
    tops_ref,
    ops_ref,
    l2l_ref,
    harmonics_ref,
    near_ref,
    out_ref,
    table,
    tops,
    stack,
):
    columns, ncoef = ops_ref.shape
    chans, atoms = out_ref.shape
    nvec = columns // ncoef
    boxes = source_ref.shape[0] // nvec
    leaf_rows = boxes * chans
    slots = atoms // boxes
    table[...] = table_ref[...].astype(jnp.float32)
    tops[...] = tops_ref[...].astype(jnp.float32)
    for vec in range(nvec):
        for box in range(boxes):
            row = pl.multiple_of(source_ref[vec * boxes + box] * chans, chans)
            stack[box * chans : (box + 1) * chans, vec * ncoef : (vec + 1) * ncoef] = table[
                pl.ds(row, chans), :ncoef
            ]
    stack[leaf_rows:, :] = jnp.zeros((chans, stack.shape[1]), jnp.float32)

    def add_entry(entry, carry):
        row = pl.multiple_of(top_source_ref[entry] * chans, chans)
        column = top_vector_ref[entry] * ncoef
        shift = column & 127
        start = pl.multiple_of(column - shift, 128)
        wide = jnp.concatenate(
            [tops[pl.ds(row, chans), :], jnp.zeros((chans, 128), jnp.float32)], axis=1
        )
        moved = pltpu.roll(wide, shift, 1)
        stack[leaf_rows:, pl.ds(start, 256)] = stack[leaf_rows:, pl.ds(start, 256)] + moved
        return carry

    lax.fori_loop(0, top_source_ref.shape[0], add_entry, 0)
    total = jnp.zeros((leaf_rows + 2 * chans, ncoef), jnp.float32)
    for start in range(0, columns, CHUNK):
        stop = min(start + CHUNK, columns)
        values = stack[:, start:stop]
        high = values.astype(jnp.bfloat16)
        rest = (values[leaf_rows:] - high[leaf_rows:].astype(jnp.float32)).astype(jnp.bfloat16)
        total = total + jnp.dot(
            jnp.concatenate([high, rest], axis=0),
            ops_ref[start:stop, :],
            preferred_element_type=jnp.float32,
        )
    parent = (total[leaf_rows : leaf_rows + chans] + total[leaf_rows + chans :]).astype(jnp.bfloat16)
    for box in range(boxes):
        child = lax.dot_general(
            parent,
            l2l_ref[box],
            (((1,), (1,)), ((), ())),
            preferred_element_type=jnp.float32,
        )
        local = (total[box * chans : (box + 1) * chans] + child).astype(jnp.bfloat16)
        span = slice(box * slots, (box + 1) * slots)
        far = jnp.dot(local, harmonics_ref[:, span], preferred_element_type=jnp.float32)
        out_ref[:, span] = (far + near_ref[:, span]).astype(out_ref.dtype)


def field(source, top_source, top_vector, table, tops, ops, l2l_ops, harmonics, near):
    chans, atoms = near.shape
    columns, ncoef = ops.shape
    boxes = l2l_ops.shape[0]
    rows = (boxes + 1) * chans
    width = (columns // 128 + 2) * 128
    smem = pl.BlockSpec(memory_space=pltpu.SMEM)
    vmem = pl.BlockSpec(memory_space=pltpu.VMEM)
    return pl.pallas_call(
        field_kernel,
        in_specs=[smem] * 3 + [vmem] * 6,
        out_specs=vmem,
        out_shape=jax.ShapeDtypeStruct((chans, atoms), jnp.bfloat16),
        scratch_shapes=[
            pltpu.VMEM((table.shape[0], 128), jnp.float32),
            pltpu.VMEM((tops.shape[0], 128), jnp.float32),
            pltpu.VMEM((rows, width), jnp.float32),
        ],
        compiler_params=pltpu.CompilerParams(vmem_limit_bytes=56 * 1024 * 1024),
        cost_estimate=pl.CostEstimate(
            flops=2 * rows * ncoef * columns, bytes_accessed=2 * ncoef * (columns + atoms), transcendentals=0
        ),
        name="field",
    )(source, top_source, top_vector, table, tops, ops, l2l_ops, harmonics, near)


def body(
    charges,
    harmonics,
    counts,
    m2l_ops,
    m2m_ops,
    l2l_ops,
    sources,
    list_mask,
    top_sources,
    top_vectors,
    neighbours,
    edge_weights,
):
    ncoef = harmonics.shape[0]
    chans = charges.shape[0]
    box_dev = counts.shape[0]
    atom_dev = charges.shape[1]
    slots = atom_dev // box_dev
    ghost = atom_dev // 4
    position = lax.axis_index("box")
    live = jnp.arange(slots, dtype=jnp.int32)[None, :] < counts[:, None]
    masked = jnp.where(
        live[None], charges.reshape(chans, box_dev, slots), jnp.zeros((), jnp.bfloat16)
    )
    flat_masked = masked.reshape(chans, atom_dev)
    harm_box = harmonics.reshape(ncoef, box_dev, slots)
    mult = jnp.einsum("cba,kba->bck", masked, harm_box, preferred_element_type=jnp.float32).astype(
        jnp.bfloat16
    )
    top = jnp.einsum("ocl,okl->ck", mult, m2m_ops, preferred_element_type=jnp.float32).astype(
        jnp.bfloat16
    )
    rows = mult.reshape(box_dev * chans, ncoef)
    rows = jnp.pad(rows, ((0, 0), (0, 128 - ncoef)))
    top = jnp.pad(top, ((0, 0), (0, 128 - ncoef)))
    tops, rows_low, rows_high, charge_low, charge_high = exchange(
        top, rows, flat_masked[:, :ghost], flat_masked[:, atom_dev - ghost :]
    )
    last = lax.axis_size("box") - 1
    charge_low = jnp.where(position == 0, jnp.zeros((), jnp.bfloat16), charge_low)
    charge_high = jnp.where(position == last, jnp.zeros((), jnp.bfloat16), charge_high)
    ext_charges = jnp.concatenate([charge_low, flat_masked, charge_high], axis=1)
    near = near_field(ext_charges, neighbours, edge_weights)
    table = jnp.concatenate(
        [rows_low, rows, rows_high, jnp.zeros((chans, 128), jnp.bfloat16)], axis=0
    )
    local_index = sources - (position - 1) * box_dev
    local_index = jnp.where(list_mask != 0, local_index, 3 * box_dev).reshape(-1)
    row_sources = lax.dynamic_slice_in_dim(top_sources, position, 1, 0)[0]
    row_vectors = lax.dynamic_slice_in_dim(top_vectors, position, 1, 0)[0]
    return field(
        local_index, row_sources, row_vectors, table, tops, m2l_ops.T, l2l_ops, harmonics, near
    )


def solution(mesh):
    return jax.shard_map(
        body,
        mesh=mesh,
        in_specs=(
            P(None, ("sys", "box")),
            P(None, ("sys", "box")),
            P(("sys", "box")),
            P(),
            P(),
            P(),
            P(None, ("sys", "box")),
            P(None, ("sys", "box")),
            P("sys", None),
            P("sys", None),
            P(None, ("sys", "box")),
            P(None, ("sys", "box")),
        ),
        out_specs=P(None, ("sys", "box")),
        check_vma=False,
    )
```
